32 devices in a mesh: groups: 2 (over x), dom: 16 (over z, y, core).
Axes of the slice: x: 2, y: 2, z: 4, core: 2. Of those that a mesh axis runs over, the one named last changes fastest.
Arguments:
- grid_in: bfloat16 [32768, 384], P(('groups', 'dom')), parts along dimension 0, may hold values from -6 to 6
- mesh_static: bfloat16 [8192, 512], P('dom'), may hold values from -6 to 6
- block_links: int32 [128, 4], replicated, may hold values from 0 to 127, as said below
- grid_links: int32 [256], P('dom'), may hold values from 0 to 7, as said below
- w_encode: bfloat16 [384, 512], replicated, may hold values from -0.3125 to 0.3125
- w_send: bfloat16 [2, 512, 512], replicated, may hold values from -0.25 to 0.25
- w_recv: bfloat16 [2, 512, 512], replicated, may hold values from -0.25 to 0.25
- edge_bias: float32 [2, 512], replicated, may hold values from -4 to 4
- w_self: bfloat16 [2, 512, 512], replicated, may hold values from -0.25 to 0.25
- w_gathered: bfloat16 [2, 512, 512], replicated, may hold values from -0.25 to 0.25
- node_bias: float32 [2, 512], replicated, may hold values from -4 to 4
- w_out: bfloat16 [2, 512, 512], replicated, may hold values from -0.25 to 0.25
- norm_gain: float32 [2, 512], replicated, may hold values from 0.5 to 2
- w_decode: bfloat16 [512, 512], replicated, may hold values from -0.25 to 0.25
- w_final: bfloat16 [512, 256], replicated, may hold values from -0.25 to 0.25
Outputs:
- prediction: float32 [32768, 256], P(('groups', 'dom')), parts along dimension 0
The draws below stay inside these ranges and needn't reach their ends.
There are 2 independent parts, one for each index of `groups`. The reference program is written for one: setup_inputs(seed, part) draws one part's arguments, and reference() takes and returns one part's arrays. A program takes and returns all parts, laid end to end along the dimension named above; an argument that names none is the same for every part. Nothing has to cross between parts.
Inputs may be any that keep to these rules, and one draw needn't show every extreme that they name: `block_links`: every named block is a block of the same partition (ids p * 8 to p * 8 + 7) or one of the first 3 blocks of the partition whose index differs by 1 or 2, counted cyclically over the partitions; a partition names at most 2 distinct blocks of each such neighbour, and exactly 2 for some pair. `grid_links`: every mesh block of a partition is tied to one or more grid blocks of that partition.
All inputs are finite; a program needn't handle non-finite values.
Results may differ from the reference program's by a relative error of at most 0.009.
Values may be sent and summed in bfloat16 or wider, within the bound.
A program may use at most 64 MiB of HBM per device.

```python
import math
import jax
import jax.numpy as jnp
from jax import lax

D = 512
FIN = 384
FOUT = 256
BLOCK = 64
K = 4
NBD = 3
CAP = 2
LAYERS = 2
MB = 8
GB = 16
MBLK = 128
MESH = 8192
GBLK = 256
GRID = 16384


def draw_grid_links(key, part):
    key = jax.random.fold_in(key, 11)
    first, second, third = jax.random.split(key, 3)
    ndevices = GBLK // GB
    covered = jax.vmap(lambda sub: jax.random.permutation(sub, MB))(jax.random.split(first, ndevices))
    extra = jax.random.randint(second, (ndevices, GB - MB), 0, MB)
    joined = jnp.concatenate([covered, extra], axis=1)
    shuffled = jax.vmap(lambda sub, row: jax.random.permutation(sub, row))(jax.random.split(third, ndevices), joined)
    return shuffled.reshape(-1).astype(jnp.int32)


def draw_block_links(key, part):
    key = jax.random.fold_in(key, 23)
    keys = jax.random.split(key, 5)
    ndevices = MBLK // MB
    owners = jnp.arange(MBLK, dtype=jnp.int32) // MB * MB
    base = owners[:, None] + jax.random.randint(keys[0], (MBLK, K), 0, MB)
    counts = jax.random.randint(keys[1], (ndevices, 4), 1, CAP + 1)
    forced = jax.random.randint(keys[2], (), 0, ndevices * 4)
    counts = jnp.where(jnp.arange(ndevices * 4).reshape(ndevices, 4) == forced, CAP, counts)
    chosen = jax.vmap(lambda sub: jax.random.permutation(sub, NBD))(jax.random.split(keys[3], ndevices * 4))
    chosen = chosen.reshape(ndevices, 4, NBD)[:, :, :CAP]
    offsets = jnp.array([1, -1, 2, -2], dtype=jnp.int32)
    neighbour = (jnp.arange(ndevices, dtype=jnp.int32)[:, None] + offsets[None, :]) % ndevices
    targets = (neighbour[:, :, None] * MB + chosen).reshape(ndevices, 4 * CAP)
    active = (jnp.arange(CAP)[None, None, :] < counts[:, :, None]).reshape(ndevices, 4 * CAP)
    spots = MB * (K - 2)
    slots = jax.vmap(lambda sub: jax.random.permutation(sub, spots))(jax.random.split(keys[4], ndevices))[:, :4 * CAP]
    match = (slots[:, :, None] == jnp.arange(spots)[None, None, :]) & active[:, :, None]
    values = jnp.sum(jnp.where(match, targets[:, :, None], 0), axis=1)
    present = jnp.any(match, axis=1)
    remote_part = base[:, 2:].reshape(ndevices, spots)
    placed = jnp.where(present, values, remote_part).reshape(MBLK, K - 2)
    return jnp.concatenate([base[:, :2], placed], axis=1).astype(jnp.int32)


def level_of(own_key, dims, shards, least, high):
    loudness = 1.0
    for dim, parts in shards:
        steps = jax.random.uniform(jax.random.fold_in(jax.random.fold_in(own_key, 6), dim), (parts,), jnp.float32, least / len(shards), high / len(shards))
        loudness = loudness * jnp.repeat(jnp.exp(steps), dims[dim] // parts).reshape((-1,) + (1,) * (len(dims) - 1 - dim))
    return loudness


def noise(key, extent, deviation, most, shards=(), kind=jnp.bfloat16):
    factor_of = level_of(key, extent, shards, -0.22, 0.18) if shards else 1.0
    values = jax.random.normal(key, extent, jnp.float32) * deviation * factor_of
    return jnp.minimum(jnp.maximum(values, -most), most).astype(kind)


def setup_inputs(seed: int = 0, part: int = 0) -> dict:
    key_list = jax.random.split(jax.random.key(seed), 16)
    part_keys = jax.random.split(jax.random.fold_in(key_list[15], part), 16)
    grid_in = noise(part_keys[0], (GRID, FIN), 1.0, 6.0, ((0, 16),))
    mesh_static = noise(key_list[1], (MESH, D), 1.0, 6.0, ((0, 16),))
    block_links = draw_block_links(jax.random.fold_in(key_list[15], 71), part)
    grid_links = draw_grid_links(jax.random.fold_in(key_list[15], 71), part)
    w_encode = noise(key_list[4], (FIN, D), FIN ** -0.5, 0.3125)
    w_send = noise(key_list[5], (LAYERS, D, D), D ** -0.5, 0.25)
    w_recv = noise(key_list[6], (LAYERS, D, D), D ** -0.5, 0.25)
    edge_bias = noise(key_list[7], (LAYERS, D), 1.0, 4.0, (), jnp.float32)
    w_self = noise(key_list[8], (LAYERS, D, D), D ** -0.5, 0.25)
    w_gathered = noise(key_list[9], (LAYERS, D, D), D ** -0.5, 0.25)
    node_bias = noise(key_list[10], (LAYERS, D), 1.0, 4.0, (), jnp.float32)
    w_out = noise(key_list[11], (LAYERS, D, D), D ** -0.5, 0.25)
    norm_gain = jnp.clip(jnp.exp(jax.random.uniform(key_list[12], (LAYERS, D), jnp.float32, math.log(0.5), math.log(2.0))), 0.5, 2.0)
    w_decode = noise(key_list[13], (D, D), D ** -0.5, 0.25)
    w_final = noise(key_list[14], (D, FOUT), D ** -0.5, 0.25)
    return {"grid_in": grid_in, "mesh_static": mesh_static, "block_links": block_links, "grid_links": grid_links, "w_encode": w_encode, "w_send": w_send, "w_recv": w_recv, "edge_bias": edge_bias, "w_self": w_self, "w_gathered": w_gathered, "node_bias": node_bias, "w_out": w_out, "norm_gain": norm_gain, "w_decode": w_decode, "w_final": w_final}


def process(state, block_links, w_send, w_recv, edge_bias, w_self, w_gathered, node_bias, w_out, norm_gain):
    f32 = jnp.float32
    source = jnp.dot(state, w_send, preferred_element_type=f32).reshape(MBLK, 1, BLOCK, D)
    tiles = state.reshape(MBLK, BLOCK, D)
    neighbours = tiles[block_links]
    projected_in = jnp.dot(neighbours.reshape(-1, D), w_recv, preferred_element_type=f32).reshape(MBLK, K, BLOCK, D)
    edges = jax.nn.silu(source + projected_in + edge_bias)
    gathered = lax.optimization_barrier(jnp.sum(edges, axis=1)).reshape(MESH, D).astype(jnp.bfloat16)
    update = jax.nn.silu(jnp.dot(state, w_self, preferred_element_type=f32) + jnp.dot(gathered, w_gathered, preferred_element_type=f32) + node_bias).astype(jnp.bfloat16)
    projected = jnp.dot(update, w_out, preferred_element_type=f32)
    center = lax.optimization_barrier(jnp.mean(projected, axis=-1, keepdims=True))
    spread = lax.optimization_barrier(jnp.mean((projected - center) ** 2, axis=-1, keepdims=True))
    normed = (projected - center) / jnp.sqrt(spread + 1e-05) * norm_gain
    return (state.astype(f32) + normed).astype(jnp.bfloat16)

def reference(grid_in, mesh_static, block_links, grid_links, w_encode, w_send, w_recv, edge_bias, w_self, w_gathered, node_bias, w_out, norm_gain, w_decode, w_final):
    f32 = jnp.float32
    encoded = jax.nn.silu(jnp.dot(grid_in, w_encode, preferred_element_type=f32)).astype(jnp.bfloat16)
    target = jnp.arange(GBLK, dtype=jnp.int32) // GB * MB + grid_links.astype(jnp.int32)
    mesh_sum = jax.ops.segment_sum(encoded.reshape(GBLK, BLOCK * D).astype(f32), target, num_segments=MBLK).reshape(MESH, D)
    state = (mesh_static.astype(f32) + mesh_sum).astype(jnp.bfloat16)
    for layer in range(LAYERS):
        state = process(state, block_links, w_send[layer], w_recv[layer], edge_bias[layer], w_self[layer], w_gathered[layer], node_bias[layer], w_out[layer], norm_gain[layer])
    tied = state.reshape(MBLK, BLOCK, D)[target].reshape(GRID, D)
    decoded = jax.nn.silu(jnp.dot(tied, w_decode, preferred_element_type=f32) + encoded.astype(f32)).astype(jnp.bfloat16)
    return jnp.dot(decoded, w_final, preferred_element_type=f32)
```

```python
import functools

import jax
import jax.numpy as jnp
from jax import lax
from jax.experimental import pallas as pl
from jax.experimental.pallas import tpu as pltpu
from jax.sharding import PartitionSpec as P

BLOCK = 64
K = 4
NBD = 3
CAP = 2
LAYERS = 2
OFFSETS = (1, -1, 2, -2)
HALF = 4
CHUNK = 16
MESH_ID = pl.DeviceIdType.MESH


def dot(a, b):
    return jnp.dot(a, b, preferred_element_type=jnp.float32)


def silu_of_half(h):
    return h + h * jnp.tanh(h)


def span(values, owner, blocks):
    low, high = NBD - 1, 0
    for value in values:
        within = value - owner * blocks
        named = (within >= 0) & (within < blocks)
        low = jnp.where(named, jnp.minimum(low, within), low)
        high = jnp.where(named, jnp.maximum(high, within), high)
    return low, high


def kernel(
    n,
    blocks,
    grid_blocks,
    grid_links,
    links,
    grid_hbm,
    static_hbm,
    *refs,
):
    weights_hbm = refs[:11]
    out_hbm = refs[11]
    (
        grid_in,
        static,
        w_encode,
        w_send,
        w_recv,
        edge_bias,
        w_self,
        w_gathered,
        node_bias,
        w_out,
        norm_gain,
        w_decode,
        w_final,
        encoded,
        state,
        source,
        own,
        table,
        gathered,
        stage,
        arrived,
        out,
        where_row,
        w_sem,
        layer_sem,
        grid_sem,
        out_sem,
        send_sem,
        recv_sem,
    ) = refs[12:]
    me = lax.axis_index("dom")
    sides = [lax.rem(me + offset + n, n) for offset in OFFSETS]
    rows = blocks * BLOCK
    grid_rows = grid_blocks * BLOCK
    half = HALF * BLOCK
    width = state.shape[3]

    barrier = pltpu.get_barrier_semaphore()
    for side in sides:
        pl.semaphore_signal(barrier, inc=1, device_id={"dom": side}, device_id_type=MESH_ID)

    copies = {}

    def fetch(name, src, dst, sem):
        copies[name] = pltpu.make_async_copy(src, dst, sem)
        copies[name].start()

    (
        w_encode_h,
        w_send_h,
        w_recv_h,
        edge_bias_h,
        w_self_h,
        w_gathered_h,
        node_bias_h,
        w_out_h,
        norm_gain_h,
        w_decode_h,
        w_final_h,
    ) = weights_hbm
    fetch("w_encode", w_encode_h, w_encode, w_sem.at[0])
    for first in range(0, grid_rows, half):
        piece = pl.ds(first, half)
        fetch(("grid", first), grid_hbm.at[piece], grid_in.at[piece], grid_sem.at[first // half])
    fetch("static", static_hbm, static, w_sem.at[1])
    fetch("edge_bias", edge_bias_h, edge_bias, w_sem.at[2])
    fetch("node_bias", node_bias_h, node_bias, w_sem.at[3])
    fetch("norm_gain", norm_gain_h, norm_gain, w_sem.at[4])
    for layer in range(LAYERS):
        for number, (src, dst) in enumerate(
            (
                (w_send_h, w_send),
                (w_recv_h, w_recv),
                (w_self_h, w_self),
                (w_gathered_h, w_gathered),
                (w_out_h, w_out),
            )
        ):
            fetch(("layer", layer, number), src.at[layer], dst.at[layer], layer_sem.at[layer, number])
    fetch("w_decode", w_decode_h, w_decode, w_sem.at[5])
    fetch("w_final", w_final_h, w_final, w_sem.at[6])

    def rows_of(owner):
        return [links[k, owner * blocks + b] for b in range(blocks) for k in range(K)]

    wanted = [span(rows_of(side), me, blocks) for side in sides]
    named = [span(rows_of(me), side, blocks) for side in sides]
    for b in range(blocks):
        for k in range(K):
            value = links[k, me * blocks + b]
            row = jnp.clip(value - me * blocks, 0, blocks - 1)
            for number, side in enumerate(sides):
                within = value - side * blocks
                theirs = (within >= 0) & (within < blocks)
                slot = jnp.where(within == named[number][0], 0, 1)
                row = jnp.where(theirs, blocks + number * CAP + slot, row)
            where_row[b * K + k] = row

    copies["w_encode"].wait()
    for first in range(0, grid_rows, half):
        copies["grid", first].wait()
        piece = pl.ds(first, half)
        encoded[piece] = silu_of_half(0.5 * dot(grid_in[piece], w_encode[...])).astype(jnp.bfloat16)

    column = lax.broadcasted_iota(jnp.int32, (8, grid_rows), 1)
    key = jnp.zeros((8, grid_rows), jnp.int32)
    for g in range(grid_blocks):
        key = jnp.where(column // BLOCK == g, grid_links[g] * BLOCK - g * BLOCK, key)
    key = (key + column)[:1]
    copies["static"].wait()

    sends = {}

    def ship(layer):
        for number, side in enumerate(sides):
            for slot in range(CAP):
                stage[layer, number, slot] = state[layer, wanted[number][slot]]
            sends[layer, number] = pltpu.make_async_remote_copy(
                src_ref=stage.at[layer, number],
                dst_ref=arrived.at[layer, number ^ 1],
                send_sem=send_sem.at[layer, number],
                recv_sem=recv_sem.at[layer, number ^ 1],
                device_id={"dom": side},
                device_id_type=MESH_ID,
            )
            sends[layer, number].start()

    for first in range(0, rows, half):
        piece = pl.ds(first, half)
        line = lax.broadcasted_iota(jnp.int32, (half, grid_rows), 0) + first
        spreader = jnp.where(line == key, 1.0, 0.0).astype(jnp.bfloat16)
        mesh_sum = dot(spreader, encoded[...])
        fresh = (static[piece].astype(jnp.float32) + mesh_sum).astype(jnp.bfloat16)
        state[0, first // BLOCK : first // BLOCK + HALF] = fresh.reshape(HALF, BLOCK, width)
        if first == 0:
            pl.semaphore_wait(barrier, len(OFFSETS))
            ship(0)

    copies["edge_bias"].wait()
    copies["node_bias"].wait()
    copies["norm_gain"].wait()
    for layer in range(LAYERS):
        copies["layer", layer, 0].wait()
        now = state[layer].reshape(rows, width)
        source[...] = 0.5 * dot(now, w_send[layer]) + 0.5 * edge_bias[layer : layer + 1]
        copies["layer", layer, 1].wait()
        table[:blocks] = (0.5 * dot(now, w_recv[layer])).reshape(blocks, BLOCK, width)
        copies["layer", layer, 2].wait()
        own[...] = 0.5 * dot(now, w_self[layer]) + 0.5 * node_bias[layer : layer + 1]
        for number in range(len(OFFSETS)):
            sends[layer, number].wait_recv()
        theirs = arrived[layer].reshape(-1, width)
        table[blocks:] = (0.5 * dot(theirs, w_recv[layer])).reshape(-1, BLOCK, width)
        copies["layer", layer, 3].wait()
        copies["layer", layer, 4].wait()
        for first in range(0, blocks, HALF):

            def edges(b, carry):
                for chunk in range(0, BLOCK, CHUNK):
                    at = pl.ds(pl.multiple_of(b * BLOCK, BLOCK) + chunk, CHUNK)
                    mine = source[at]
                    total = None
                    for k in range(K):
                        row = where_row[b * K + k]
                        h = mine + table[row, chunk : chunk + CHUNK]
                        edge = silu_of_half(h)
                        total = edge if total is None else total + edge
                    gathered[at] = total.astype(jnp.bfloat16)
                return carry

            lax.fori_loop(first, first + HALF, edges, 0)
            piece = pl.ds(first * BLOCK, half)
            update = silu_of_half(own[piece] + 0.5 * dot(gathered[piece], w_gathered[layer]))
            projected = dot(update.astype(jnp.bfloat16), w_out[layer])
            center = jnp.mean(projected, axis=-1, keepdims=True)
            away = projected - center
            spread = jnp.mean(away * away, axis=-1, keepdims=True)
            normed = away * lax.rsqrt(spread + 1e-05) * norm_gain[layer : layer + 1]
            tiles = slice(first, first + HALF)
            before = state[layer, tiles].reshape(half, width).astype(jnp.float32)
            state[layer + 1, tiles] = (
                (before + normed).astype(jnp.bfloat16).reshape(HALF, BLOCK, width)
            )
            if first == 0 and layer + 1 < LAYERS:
                ship(layer + 1)

    copies["w_decode"].wait()
    table[:blocks] = (0.5 * dot(state[LAYERS].reshape(rows, width), w_decode[...])).reshape(
        blocks, BLOCK, width
    )
    copies["w_final"].wait()
    writes = []
    for first in range(0, grid_rows, half):
        for g in range(first // BLOCK, (first + half) // BLOCK):
            at = pl.ds(g * BLOCK, BLOCK)
            tied = table[grid_links[g]]
            encoded[at] = silu_of_half(tied + 0.5 * encoded[at].astype(jnp.float32)).astype(
                jnp.bfloat16
            )
        piece = pl.ds(first, half)
        out[piece] = dot(encoded[piece], w_final[...])
        write = pltpu.make_async_copy(out.at[piece], out_hbm.at[piece], out_sem.at[first // half])
        write.start()
        writes.append(write)
    for write in writes:
        write.wait()
    for copy in sends.values():
        copy.wait_send()


def local(grid_in, mesh_static, block_links, grid_links, *weights):
    bf16, f32 = jnp.bfloat16, jnp.float32
    n = lax.axis_size("dom")
    rows, width = mesh_static.shape
    blocks = rows // BLOCK
    grid_rows, fields = grid_in.shape
    grid_blocks = grid_rows // BLOCK
    remote = len(OFFSETS) * CAP
    outputs = weights[-1].shape[1]
    scratch = [
        pltpu.VMEM(grid_in.shape, bf16),
        pltpu.VMEM(mesh_static.shape, bf16),
    ]
    scratch += [pltpu.VMEM(w.shape, w.dtype) for w in weights]
    scratch += [
        pltpu.VMEM((grid_rows, width), bf16),
        pltpu.VMEM((LAYERS + 1, blocks, BLOCK, width), bf16),
        pltpu.VMEM((rows, width), f32),
        pltpu.VMEM((rows, width), f32),
        pltpu.VMEM((blocks + remote, BLOCK, width), f32),
        pltpu.VMEM((rows, width), bf16),
        pltpu.VMEM((LAYERS, len(OFFSETS), CAP, BLOCK, width), bf16),
        pltpu.VMEM((LAYERS, len(OFFSETS), CAP, BLOCK, width), bf16),
        pltpu.VMEM((grid_rows, outputs), f32),
        pltpu.SMEM((blocks * K,), jnp.int32),
        pltpu.SemaphoreType.DMA((7,)),
        pltpu.SemaphoreType.DMA((LAYERS, 5)),
        pltpu.SemaphoreType.DMA((grid_rows // (HALF * BLOCK),)),
        pltpu.SemaphoreType.DMA((grid_rows // (HALF * BLOCK),)),
        pltpu.SemaphoreType.DMA((LAYERS, len(OFFSETS))),
        pltpu.SemaphoreType.DMA((LAYERS, len(OFFSETS))),
    ]
    anywhere = pl.BlockSpec(memory_space=pl.ANY)
    return pl.pallas_call(
        functools.partial(kernel, n, blocks, grid_blocks),
        out_shape=jax.ShapeDtypeStruct((grid_rows, outputs), f32),
        in_specs=[pl.BlockSpec(memory_space=pltpu.SMEM)] * 2 + [anywhere] * (2 + len(weights)),
        out_specs=anywhere,
        scratch_shapes=scratch,
        compiler_params=pltpu.CompilerParams(
            collective_id=0, has_side_effects=True, vmem_limit_bytes=56 * 1024 * 1024
        ),
    )(grid_links, block_links.T, grid_in, mesh_static, *weights)


def solution(mesh):
    whole = P()
    split = P(("groups", "dom"), None)
    in_specs = (split, P("dom", None), whole, P("dom")) + (whole,) * 11
    return jax.shard_map(
        local, mesh=mesh, in_specs=in_specs, out_specs=split, check_vma=False
    )
```

```python
import functools

import jax
import jax.numpy as jnp
from jax import lax
from jax.experimental import pallas as pl
from jax.experimental.pallas import tpu as pltpu
from jax.sharding import PartitionSpec as P

BLOCK = 64
K = 4
NBD = 3
CAP = 2
LAYERS = 2
OFFSETS = (1, -1, 2, -2)
PARTS = 2
CHUNK = 16
MESH_ID = pl.DeviceIdType.MESH


def dot(a, b):
    return jnp.dot(a, b, preferred_element_type=jnp.float32)


def silu_of_half(h):
    return h + h * jnp.tanh(h)


def span(values, owner, blocks):
    low, high = NBD - 1, 0
    for value in values:
        within = value - owner * blocks
        named = (within >= 0) & (within < blocks)
        low = jnp.where(named, jnp.minimum(low, within), low)
        high = jnp.where(named, jnp.maximum(high, within), high)
    return low, high


def kernel(n, blocks, grid_blocks, grid_links, links, grid_hbm, static_hbm, *refs):
    weights_hbm = refs[:11]
    out_hbm = refs[11]
    weights = refs[12:23]
    (
        grid_in,
        static,
        encoded,
        state,
        source,
        own,
        table,
        gathered,
        stage,
        arrived,
        out,
        where_row,
        w_sem,
        layer_sem,
        grid_sem,
        static_sem,
        out_sem,
        send_sem,
        recv_sem,
    ) = refs[23:]
    (
        w_encode,
        w_send,
        w_recv,
        edge_bias,
        w_self,
        w_gathered,
        node_bias,
        w_out,
        norm_gain,
        w_decode,
        w_final,
    ) = weights
    me = lax.axis_index("dom")
    sides = [lax.rem(me + offset + n, n) for offset in OFFSETS]
    width = state.shape[4]
    nodes = BLOCK // PARTS
    rows = blocks * nodes
    grid_rows = grid_blocks * nodes
    f32, bf16 = jnp.float32, jnp.bfloat16

    barrier = pltpu.get_barrier_semaphore()
    for side in sides:
        pl.semaphore_signal(barrier, inc=1, device_id={"dom": side}, device_id_type=MESH_ID)

    copies = {}

    def fetch(name, src, dst, sem):
        copies[name] = pltpu.make_async_copy(src, dst, sem)
        copies[name].start()

    def fetch_weight(number):
        fetch(number, weights_hbm[number], weights[number], w_sem.at[number])

    fetch_weight(0)
    for part in range(PARTS):
        piece = pl.ds(part * nodes, nodes)
        fetch(("grid", part), grid_hbm.at[:, piece], grid_in.at[part], grid_sem.at[part])
        fetch(("static", part), static_hbm.at[:, piece], static.at[part], static_sem.at[part])
    for number in (3, 6, 8):
        fetch_weight(number)
    for layer in range(LAYERS):
        for number in (1, 2, 4, 5, 7):
            fetch(
                (layer, number),
                weights_hbm[number].at[layer],
                weights[number].at[layer],
                layer_sem.at[layer, number],
            )
    fetch_weight(9)
    fetch_weight(10)

    def rows_of(owner):
        return [links[k, owner * blocks + b] for b in range(blocks) for k in range(K)]

    wanted = [span(rows_of(side), me, blocks) for side in sides]
    named = [span(rows_of(me), side, blocks) for side in sides]
    for b in range(blocks):
        for k in range(K):
            value = links[k, me * blocks + b]
            row = jnp.clip(value - me * blocks, 0, blocks - 1)
            for number, side in enumerate(sides):
                within = value - side * blocks
                theirs = (within >= 0) & (within < blocks)
                slot = jnp.where(within == named[number][0], 0, 1)
                row = jnp.where(theirs, blocks + number * CAP + slot, row)
            where_row[b * K + k] = row

    column = lax.broadcasted_iota(jnp.int32, (8, grid_rows), 1)
    key = jnp.zeros((8, grid_rows), jnp.int32)
    for g in range(grid_blocks):
        key = jnp.where(column // nodes == g, grid_links[g] * nodes - g * nodes, key)
    key = (key + column)[:1]
    line = lax.broadcasted_iota(jnp.int32, (rows, grid_rows), 0)
    spreader = jnp.where(line == key, 1.0, 0.0).astype(bf16)

    sends = {}

    def ship(layer, part):
        for number, side in enumerate(sides):
            for slot in range(CAP):
                stage[layer, part, number, slot] = state[layer, part, wanted[number][slot]]
            send = pltpu.make_async_remote_copy(
                src_ref=stage.at[layer, part, number],
                dst_ref=arrived.at[layer, part, number ^ 1],
                send_sem=send_sem.at[layer, part, number],
                recv_sem=recv_sem.at[layer, part, number ^ 1],
                device_id={"dom": side},
                device_id_type=MESH_ID,
            )
            send.start()
            sends[layer, part, number] = send

    def encode(part):
        copies["grid", part].wait()
        fields = grid_in[part].reshape(grid_rows, -1)
        fresh = silu_of_half(0.5 * dot(fields, w_encode[...])).astype(bf16)
        encoded[part] = fresh.reshape(grid_blocks, nodes, width)
        mesh_sum = dot(spreader, fresh)
        copies["static", part].wait()
        begun = static[part].reshape(rows, width).astype(f32) + mesh_sum
        state[0, part] = begun.astype(bf16).reshape(blocks, nodes, width)

    def project(layer, part):
        now = state[layer, part].reshape(rows, width)
        source[part] = 0.5 * dot(now, w_send[layer]) + 0.5 * edge_bias[layer : layer + 1]
        table[part, :blocks] = (0.5 * dot(now, w_recv[layer])).reshape(blocks, nodes, width)
        own[part] = 0.5 * dot(now, w_self[layer]) + 0.5 * node_bias[layer : layer + 1]

    def process(layer, part):
        for number in range(len(OFFSETS)):
            sends[layer, part, number].wait_recv()
        theirs = arrived[layer, part].reshape(-1, width)
        table[part, blocks:] = (0.5 * dot(theirs, w_recv[layer])).reshape(-1, nodes, width)

        def edges(b, carry):
            for chunk in range(0, nodes, CHUNK):
                at = pl.ds(pl.multiple_of(b * nodes, nodes) + chunk, CHUNK)
                mine = source[part, at]
                total = None
                for k in range(K):
                    edge = silu_of_half(mine + table[part, where_row[b * K + k], chunk : chunk + CHUNK])
                    total = edge if total is None else total + edge
                gathered[part, at] = total.astype(bf16)
            return carry

        lax.fori_loop(0, blocks, edges, 0)
        update = silu_of_half(own[part] + 0.5 * dot(gathered[part], w_gathered[layer]))
        projected = dot(update.astype(bf16), w_out[layer])
        center = jnp.mean(projected, axis=-1, keepdims=True)
        away = projected - center
        spread = jnp.mean(away * away, axis=-1, keepdims=True)
        normed = away * lax.rsqrt(spread + 1e-05) * norm_gain[layer : layer + 1]
        before = state[layer, part].reshape(rows, width).astype(f32)
        state[layer + 1, part] = (before + normed).astype(bf16).reshape(blocks, nodes, width)

    writes = []

    def decode(part):
        last = state[LAYERS, part].reshape(rows, width)
        table[part, :blocks] = (0.5 * dot(last, w_decode[...])).reshape(blocks, nodes, width)
        for g in range(grid_blocks):
            h = table[part, grid_links[g]] + 0.5 * encoded[part, g].astype(f32)
            encoded[part, g] = silu_of_half(h).astype(bf16)
        found = dot(encoded[part].reshape(grid_rows, width), w_final[...])
        out[part] = found.reshape(grid_blocks, nodes, -1)
        write = pltpu.make_async_copy(
            out.at[part], out_hbm.at[:, pl.ds(part * nodes, nodes)], out_sem.at[part]
        )
        write.start()
        writes.append(write)

    copies[0].wait()
    for part in range(PARTS):
        encode(part)
        if part == 0:
            pl.semaphore_wait(barrier, len(OFFSETS))
        ship(0, part)
    for number in (3, 6, 8):
        copies[number].wait()
    for layer in range(LAYERS):
        for number in (1, 2, 4):
            copies[layer, number].wait()
        for part in range(PARTS):
            project(layer, part)
        for number in (5, 7):
            copies[layer, number].wait()
        if layer == LAYERS - 1:
            copies[9].wait()
            copies[10].wait()
        for part in range(PARTS):
            process(layer, part)
            if layer + 1 < LAYERS:
                ship(layer + 1, part)
            else:
                decode(part)
    for write in writes:
        write.wait()
    for send in sends.values():
        send.wait_send()


def local(grid_in, mesh_static, block_links, grid_links, *weights):
    bf16, f32 = jnp.bfloat16, jnp.float32
    n = lax.axis_size("dom")
    rows, width = mesh_static.shape
    blocks = rows // BLOCK
    grid_rows, fields = grid_in.shape
    grid_blocks = grid_rows // BLOCK
    nodes = BLOCK // PARTS
    sides = len(OFFSETS)
    outputs = weights[-1].shape[1]
    scratch = [pltpu.VMEM(w.shape, w.dtype) for w in weights]
    scratch += [
        pltpu.VMEM((PARTS, grid_blocks, nodes, fields), bf16),
        pltpu.VMEM((PARTS, blocks, nodes, width), bf16),
        pltpu.VMEM((PARTS, grid_blocks, nodes, width), bf16),
        pltpu.VMEM((LAYERS + 1, PARTS, blocks, nodes, width), bf16),
        pltpu.VMEM((PARTS, blocks * nodes, width), f32),
        pltpu.VMEM((PARTS, blocks * nodes, width), f32),
        pltpu.VMEM((PARTS, blocks + sides * CAP, nodes, width), f32),
        pltpu.VMEM((PARTS, blocks * nodes, width), bf16),
        pltpu.VMEM((LAYERS, PARTS, sides, CAP, nodes, width), bf16),
        pltpu.VMEM((LAYERS, PARTS, sides, CAP, nodes, width), bf16),
        pltpu.VMEM((PARTS, grid_blocks, nodes, outputs), f32),
        pltpu.SMEM((blocks * K,), jnp.int32),
        pltpu.SemaphoreType.DMA((len(weights),)),
        pltpu.SemaphoreType.DMA((LAYERS, len(weights))),
        pltpu.SemaphoreType.DMA((PARTS,)),
        pltpu.SemaphoreType.DMA((PARTS,)),
        pltpu.SemaphoreType.DMA((PARTS,)),
        pltpu.SemaphoreType.DMA((LAYERS, PARTS, sides)),
        pltpu.SemaphoreType.DMA((LAYERS, PARTS, sides)),
    ]
    anywhere = pl.BlockSpec(memory_space=pl.ANY)
    found = pl.pallas_call(
        functools.partial(kernel, n, blocks, grid_blocks),
        out_shape=jax.ShapeDtypeStruct((grid_blocks, BLOCK, outputs), f32),
        in_specs=[pl.BlockSpec(memory_space=pltpu.SMEM)] * 2 + [anywhere] * (2 + len(weights)),
        out_specs=anywhere,
        scratch_shapes=scratch,
        compiler_params=pltpu.CompilerParams(
            collective_id=0, has_side_effects=True, vmem_limit_bytes=56 * 1024 * 1024
        ),
    )(
        grid_links,
        block_links.T,
        grid_in.reshape(grid_blocks, BLOCK, fields),
        mesh_static.reshape(blocks, BLOCK, width),
        *weights,
    )
    return found.reshape(grid_rows, outputs)


def solution(mesh):
    whole = P()
    split = P(("groups", "dom"), None)
    in_specs = (split, P("dom", None), whole, P("dom")) + (whole,) * 11
    return jax.shard_map(
        local, mesh=mesh, in_specs=in_specs, out_specs=split, check_vma=False
    )
```

```python
import functools

import jax
import jax.numpy as jnp
from jax import lax
from jax.experimental import pallas as pl
from jax.experimental.pallas import tpu as pltpu
from jax.sharding import PartitionSpec as P

BLOCK = 64
K = 4
NBD = 3
CAP = 2
LAYERS = 2
NEAR, RELAY, PARTNER, FAR = range(4)
BASE = (0, NBD, 2 * NBD, 2 * NBD + CAP)
REMOTE = 2 * (NBD + CAP)
PARTS = 2
CHUNK = 16
MESH_ID = pl.DeviceIdType.MESH


def dot(a, b):
    return jnp.dot(a, b, preferred_element_type=jnp.float32)


def silu_of_half(h):
    return h + h * jnp.tanh(h)


def span(values, owner, blocks):
    low, high = NBD - 1, 0
    for value in values:
        within = value - owner * blocks
        named = (within >= 0) & (within < blocks)
        low = jnp.where(named, jnp.minimum(low, within), low)
        high = jnp.where(named, jnp.maximum(high, within), high)
    return low, high


def kernel(n, blocks, grid_blocks, grid_links, links, grid_hbm, static_hbm, *refs):
    weights_hbm = refs[:11]
    out_hbm = refs[11]
    weights = refs[12:23]
    (
        grid_in,
        static,
        encoded,
        state,
        source,
        own,
        table,
        gathered,
        stage,
        arrived,
        out,
        where_row,
        w_sem,
        layer_sem,
        grid_sem,
        static_sem,
        out_sem,
        send_sem,
        recv_sem,
    ) = refs[23:]
    (
        w_encode,
        w_send,
        w_recv,
        edge_bias,
        w_self,
        w_gathered,
        node_bias,
        w_out,
        norm_gain,
        w_decode,
        w_final,
    ) = weights
    me = lax.axis_index("dom")
    toward = 2 * lax.rem(me, 2) - 1
    near = lax.rem(me + toward + n, n)
    behind = lax.rem(me - 2 * toward + n, n)
    partner = lax.rem(me - toward + n, n)
    ahead = lax.rem(me + 2 * toward + n, n)
    sides = (near, behind, partner, ahead)
    width = state.shape[4]
    nodes = BLOCK // PARTS
    rows = blocks * nodes
    grid_rows = grid_blocks * nodes
    f32, bf16 = jnp.float32, jnp.bfloat16

    barrier = pltpu.get_barrier_semaphore()
    for side in sides:
        pl.semaphore_signal(barrier, inc=1, device_id={"dom": side}, device_id_type=MESH_ID)

    copies = {}

    def fetch(name, src, dst, sem):
        copies[name] = pltpu.make_async_copy(src, dst, sem)
        copies[name].start()

    def fetch_weight(number):
        fetch(number, weights_hbm[number], weights[number], w_sem.at[number])

    fetch_weight(0)
    for part in range(PARTS):
        piece = pl.ds(part * nodes, nodes)
        fetch(("grid", part), grid_hbm.at[:, piece], grid_in.at[part], grid_sem.at[part])
        fetch(("static", part), static_hbm.at[:, piece], static.at[part], static_sem.at[part])
    for number in (3, 6, 8):
        fetch_weight(number)
    for layer in range(LAYERS):
        for number in (1, 2, 4, 5, 7):
            fetch(
                (layer, number),
                weights_hbm[number].at[layer],
                weights[number].at[layer],
                layer_sem.at[layer, number],
            )
    fetch_weight(9)
    fetch_weight(10)

    def rows_of(owner):
        return [links[k, owner * blocks + b] for b in range(blocks) for k in range(K)]

    wanted = {PARTNER: span(rows_of(partner), me, blocks), FAR: span(rows_of(behind), me, blocks)}
    named = {number: span(rows_of(me), sides[number], blocks) for number in (PARTNER, FAR)}
    for b in range(blocks):
        for k in range(K):
            value = links[k, me * blocks + b]
            row = jnp.clip(value - me * blocks, 0, blocks - 1)
            for number, side in enumerate(sides):
                within = value - side * blocks
                theirs = (within >= 0) & (within < blocks)
                if number in named:
                    slot = jnp.where(within == named[number][0], 0, 1)
                else:
                    slot = jnp.clip(within, 0, NBD - 1)
                row = jnp.where(theirs, blocks + BASE[number] + slot, row)
            where_row[b * K + k] = row

    column = lax.broadcasted_iota(jnp.int32, (8, grid_rows), 1)
    key = jnp.zeros((8, grid_rows), jnp.int32)
    for g in range(grid_blocks):
        key = jnp.where(column // nodes == g, grid_links[g] * nodes - g * nodes, key)
    key = (key + column)[:1]
    line = lax.broadcasted_iota(jnp.int32, (rows, grid_rows), 0)
    spreader = jnp.where(line == key, 1.0, 0.0).astype(bf16)

    sends = {}

    def send(layer, part, number, src, side, count):
        copy = pltpu.make_async_remote_copy(
            src_ref=src,
            dst_ref=arrived.at[layer, part, pl.ds(BASE[number], count)],
            send_sem=send_sem.at[layer, part, number],
            recv_sem=recv_sem.at[layer, part, number],
            device_id={"dom": side},
            device_id_type=MESH_ID,
        )
        copy.start()
        sends[layer, part, number] = copy

    def ship(layer, part):
        send(layer, part, NEAR, state.at[layer, part, pl.ds(0, NBD)], near, NBD)
        for number, side in ((FAR, behind), (PARTNER, partner)):
            for slot in range(CAP):
                stage[layer, part, number - PARTNER, slot] = state[layer, part, wanted[number][slot]]
            send(layer, part, number, stage.at[layer, part, number - PARTNER], side, CAP)

    def encode(part):
        copies["grid", part].wait()
        fields = grid_in[part].reshape(grid_rows, -1)
        fresh = silu_of_half(0.5 * dot(fields, w_encode[...])).astype(bf16)
        encoded[part] = fresh.reshape(grid_blocks, nodes, width)
        mesh_sum = dot(spreader, fresh)
        copies["static", part].wait()
        begun = static[part].reshape(rows, width).astype(f32) + mesh_sum
        state[0, part] = begun.astype(bf16).reshape(blocks, nodes, width)

    def project(layer, part):
        now = state[layer, part].reshape(rows, width)
        source[part] = 0.5 * dot(now, w_send[layer]) + 0.5 * edge_bias[layer : layer + 1]
        table[part, :blocks] = (0.5 * dot(now, w_recv[layer])).reshape(blocks, nodes, width)
        own[part] = 0.5 * dot(now, w_self[layer]) + 0.5 * node_bias[layer : layer + 1]

    def process(layer, part):
        sends[layer, part, NEAR].wait_recv()
        passed = arrived.at[layer, part, pl.ds(BASE[NEAR], NBD)]
        send(layer, part, RELAY, passed, partner, NBD)
        for number in (PARTNER, FAR, RELAY):
            sends[layer, part, number].wait_recv()
        theirs = arrived[layer, part].reshape(-1, width)
        table[part, blocks:] = (0.5 * dot(theirs, w_recv[layer])).reshape(-1, nodes, width)

        def edges(b, carry):
            for chunk in range(0, nodes, CHUNK):
                at = pl.ds(pl.multiple_of(b * nodes, nodes) + chunk, CHUNK)
                mine = source[part, at]
                total = None
                for k in range(K):
                    edge = silu_of_half(mine + table[part, where_row[b * K + k], chunk : chunk + CHUNK])
                    total = edge if total is None else total + edge
                gathered[part, at] = total.astype(bf16)
            return carry

        lax.fori_loop(0, blocks, edges, 0)
        update = silu_of_half(own[part] + 0.5 * dot(gathered[part], w_gathered[layer]))
        projected = dot(update.astype(bf16), w_out[layer])
        center = jnp.mean(projected, axis=-1, keepdims=True)
        away = projected - center
        spread = jnp.mean(away * away, axis=-1, keepdims=True)
        normed = away * lax.rsqrt(spread + 1e-05) * norm_gain[layer : layer + 1]
        before = state[layer, part].reshape(rows, width).astype(f32)
        state[layer + 1, part] = (before + normed).astype(bf16).reshape(blocks, nodes, width)

    writes = []

    def decode(part):
        last = state[LAYERS, part].reshape(rows, width)
        table[part, :blocks] = (0.5 * dot(last, w_decode[...])).reshape(blocks, nodes, width)
        for g in range(grid_blocks):
            h = table[part, grid_links[g]] + 0.5 * encoded[part, g].astype(f32)
            encoded[part, g] = silu_of_half(h).astype(bf16)
        found = dot(encoded[part].reshape(grid_rows, width), w_final[...])
        out[part] = found.reshape(grid_blocks, nodes, -1)
        write = pltpu.make_async_copy(
            out.at[part], out_hbm.at[:, pl.ds(part * nodes, nodes)], out_sem.at[part]
        )
        write.start()
        writes.append(write)

    copies[0].wait()
    for part in range(PARTS):
        encode(part)
        if part == 0:
            pl.semaphore_wait(barrier, len(sides))
        ship(0, part)
    for number in (3, 6, 8):
        copies[number].wait()
    for layer in range(LAYERS):
        for number in (1, 2, 4):
            copies[layer, number].wait()
        for part in range(PARTS):
            project(layer, part)
        for number in (5, 7):
            copies[layer, number].wait()
        if layer == LAYERS - 1:
            copies[9].wait()
            copies[10].wait()
        for part in range(PARTS):
            process(layer, part)
            if layer + 1 < LAYERS:
                ship(layer + 1, part)
            else:
                decode(part)
    for write in writes:
        write.wait()
    for copy in sends.values():
        copy.wait_send()


def local(grid_in, mesh_static, block_links, grid_links, *weights):
    bf16, f32 = jnp.bfloat16, jnp.float32
    n = lax.axis_size("dom")
    rows, width = mesh_static.shape
    blocks = rows // BLOCK
    grid_rows, fields = grid_in.shape
    grid_blocks = grid_rows // BLOCK
    nodes = BLOCK // PARTS
    outputs = weights[-1].shape[1]
    scratch = [pltpu.VMEM(w.shape, w.dtype) for w in weights]
    scratch += [
        pltpu.VMEM((PARTS, grid_blocks, nodes, fields), bf16),
        pltpu.VMEM((PARTS, blocks, nodes, width), bf16),
        pltpu.VMEM((PARTS, grid_blocks, nodes, width), bf16),
        pltpu.VMEM((LAYERS + 1, PARTS, blocks, nodes, width), bf16),
        pltpu.VMEM((PARTS, blocks * nodes, width), f32),
        pltpu.VMEM((PARTS, blocks * nodes, width), f32),
        pltpu.VMEM((PARTS, blocks + REMOTE, nodes, width), f32),
        pltpu.VMEM((PARTS, blocks * nodes, width), bf16),
        pltpu.VMEM((LAYERS, PARTS, 2, CAP, nodes, width), bf16),
        pltpu.VMEM((LAYERS, PARTS, REMOTE, nodes, width), bf16),
        pltpu.VMEM((PARTS, grid_blocks, nodes, outputs), f32),
        pltpu.SMEM((blocks * K,), jnp.int32),
        pltpu.SemaphoreType.DMA((len(weights),)),
        pltpu.SemaphoreType.DMA((LAYERS, len(weights))),
        pltpu.SemaphoreType.DMA((PARTS,)),
        pltpu.SemaphoreType.DMA((PARTS,)),
        pltpu.SemaphoreType.DMA((PARTS,)),
        pltpu.SemaphoreType.DMA((LAYERS, PARTS, 4)),
        pltpu.SemaphoreType.DMA((LAYERS, PARTS, 4)),
    ]
    anywhere = pl.BlockSpec(memory_space=pl.ANY)
    found = pl.pallas_call(
        functools.partial(kernel, n, blocks, grid_blocks),
        out_shape=jax.ShapeDtypeStruct((grid_blocks, BLOCK, outputs), f32),
        in_specs=[pl.BlockSpec(memory_space=pltpu.SMEM)] * 2 + [anywhere] * (2 + len(weights)),
        out_specs=anywhere,
        scratch_shapes=scratch,
        compiler_params=pltpu.CompilerParams(
            collective_id=0, has_side_effects=True, vmem_limit_bytes=56 * 1024 * 1024
        ),
    )(
        grid_links,
        block_links.T,
        grid_in.reshape(grid_blocks, BLOCK, fields),
        mesh_static.reshape(blocks, BLOCK, width),
        *weights,
    )
    return found.reshape(grid_rows, outputs)


def solution(mesh):
    whole = P()
    split = P(("groups", "dom"), None)
    in_specs = (split, P("dom", None), whole, P("dom")) + (whole,) * 11
    return jax.shard_map(
        local, mesh=mesh, in_specs=in_specs, out_specs=split, check_vma=False
    )
```

```python
import functools

import jax
import jax.numpy as jnp
from jax import lax
from jax.experimental import pallas as pl
from jax.experimental.pallas import tpu as pltpu
from jax.sharding import PartitionSpec as P

BLOCK = 64
K = 4
NBD = 3
CAP = 2
LAYERS = 2
NEAR, RELAY, PARTNER, FAR = range(4)
BASE = (0, NBD, 2 * NBD, 2 * NBD + CAP)
REMOTE = 2 * (NBD + CAP)
PARTS = 2
CHUNK = 16
MESH_ID = pl.DeviceIdType.MESH


def dot(a, b):
    return jnp.dot(a, b, preferred_element_type=jnp.float32)


def silu_of_half(h):
    return h + h * jnp.tanh(h)


def span(values, owner, blocks):
    low, high = NBD - 1, 0
    for value in values:
        within = value - owner * blocks
        named = (within >= 0) & (within < blocks)
        low = jnp.where(named, jnp.minimum(low, within), low)
        high = jnp.where(named, jnp.maximum(high, within), high)
    return low, high


def kernel(n, blocks, grid_blocks, grid_links, links, grid_hbm, static_hbm, *refs):
    weights_hbm = refs[:11]
    out_hbm = refs[11]
    weights = refs[12:23]
    (
        grid_in,
        static,
        encoded,
        state,
        source,
        own,
        table,
        gathered,
        stage,
        arrived,
        out,
        where_row,
        w_sem,
        layer_sem,
        grid_sem,
        static_sem,
        out_sem,
        send_sem,
        recv_sem,
    ) = refs[23:]
    (
        w_encode,
        w_send,
        w_recv,
        edge_bias,
        w_self,
        w_gathered,
        node_bias,
        w_out,
        norm_gain,
        w_decode,
        w_final,
    ) = weights
    me = lax.axis_index("dom")
    toward = 2 * lax.rem(me, 2) - 1
    near = lax.rem(me + toward + n, n)
    behind = lax.rem(me - 2 * toward + n, n)
    partner = lax.rem(me - toward + n, n)
    ahead = lax.rem(me + 2 * toward + n, n)
    sides = (near, behind, partner, ahead)
    width = state.shape[4]
    nodes = BLOCK // PARTS
    rows = blocks * nodes
    grid_rows = grid_blocks * nodes
    f32, bf16 = jnp.float32, jnp.bfloat16

    barrier = pltpu.get_barrier_semaphore()
    for side in sides:
        pl.semaphore_signal(barrier, inc=1, device_id={"dom": side}, device_id_type=MESH_ID)

    copies = {}

    def fetch(name, src, dst, sem):
        copies[name] = pltpu.make_async_copy(src, dst, sem)
        copies[name].start()

    def fetch_weight(number):
        fetch(number, weights_hbm[number], weights[number], w_sem.at[number])

    fetch_weight(0)
    for part in range(PARTS):
        piece = pl.ds(part * nodes, nodes)
        fetch(("grid", part), grid_hbm.at[:, piece], grid_in.at[part], grid_sem.at[part])
        fetch(("static", part), static_hbm.at[:, piece], static.at[part], static_sem.at[part])
    for number in (3, 6, 8):
        fetch_weight(number)
    for layer in range(LAYERS):
        for number in (1, 2, 4, 5, 7):
            fetch(
                (layer, number),
                weights_hbm[number].at[layer],
                weights[number].at[layer],
                layer_sem.at[layer, number],
            )
    fetch_weight(9)
    fetch_weight(10)

    def rows_of(owner):
        return [links[k, owner * blocks + b] for b in range(blocks) for k in range(K)]

    wanted = {PARTNER: span(rows_of(partner), me, blocks), FAR: span(rows_of(behind), me, blocks)}
    named = {number: span(rows_of(me), sides[number], blocks) for number in (PARTNER, FAR)}
    for b in range(blocks):
        for k in range(K):
            value = links[k, me * blocks + b]
            row = jnp.clip(value - me * blocks, 0, blocks - 1)
            for number, side in enumerate(sides):
                within = value - side * blocks
                theirs = (within >= 0) & (within < blocks)
                if number in named:
                    slot = jnp.where(within == named[number][0], 0, 1)
                else:
                    slot = jnp.clip(within, 0, NBD - 1)
                row = jnp.where(theirs, blocks + BASE[number] + slot, row)
            where_row[b * K + k] = row

    column = lax.broadcasted_iota(jnp.int32, (8, grid_rows), 1)
    key = jnp.zeros((8, grid_rows), jnp.int32)
    for g in range(grid_blocks):
        key = jnp.where(column // nodes == g, grid_links[g] * nodes - g * nodes, key)
    key = (key + column)[:1]
    line = lax.broadcasted_iota(jnp.int32, (rows, grid_rows), 0)
    spreader = jnp.where(line == key, 1.0, 0.0).astype(bf16)

    sends = {}

    def send(layer, part, number, src, side, count):
        copy = pltpu.make_async_remote_copy(
            src_ref=src,
            dst_ref=arrived.at[layer, part, pl.ds(BASE[number], count)],
            send_sem=send_sem.at[layer, part, number],
            recv_sem=recv_sem.at[layer, part, number],
            device_id={"dom": side},
            device_id_type=MESH_ID,
        )
        copy.start()
        sends[layer, part, number] = copy

    def ship(layer, part):
        send(layer, part, NEAR, state.at[layer, part, pl.ds(0, NBD)], near, NBD)
        for number, side in ((FAR, behind), (PARTNER, partner)):
            for slot in range(CAP):
                stage[layer, part, number - PARTNER, slot] = state[layer, part, wanted[number][slot]]
            send(layer, part, number, stage.at[layer, part, number - PARTNER], side, CAP)

    def encode(part):
        copies["grid", part].wait()
        fields = grid_in[part].reshape(grid_rows, -1)
        fresh = silu_of_half(0.5 * dot(fields, w_encode[...])).astype(bf16)
        encoded[part] = fresh.reshape(grid_blocks, nodes, width)
        mesh_sum = dot(spreader, fresh)
        copies["static", part].wait()
        begun = static[part].reshape(rows, width).astype(f32) + mesh_sum
        state[0, part] = begun.astype(bf16).reshape(blocks, nodes, width)

    def project(layer, part):
        now = state[layer, part].reshape(rows, width)
        source[part] = 0.5 * dot(now, w_send[layer]) + 0.5 * edge_bias[layer : layer + 1]
        table[part, :blocks] = (0.5 * dot(now, w_recv[layer])).reshape(blocks, nodes, width)
        own[part] = 0.5 * dot(now, w_self[layer]) + 0.5 * node_bias[layer : layer + 1]

    def process(layer, part):
        sends[layer, part, NEAR].wait_recv()
        passed = arrived.at[layer, part, pl.ds(BASE[NEAR], NBD)]
        send(layer, part, RELAY, passed, partner, NBD)
        for number in (PARTNER, FAR, RELAY):
            sends[layer, part, number].wait_recv()
        theirs = arrived[layer, part].reshape(-1, width)
        table[part, blocks:] = (0.5 * dot(theirs, w_recv[layer])).reshape(-1, nodes, width)

        def edges(b, carry):
            for chunk in range(0, nodes, CHUNK):
                at = pl.ds(pl.multiple_of(b * nodes, nodes) + chunk, CHUNK)
                mine = source[part, at]
                total = None
                for k in range(K):
                    edge = silu_of_half(mine + table[part, where_row[b * K + k], chunk : chunk + CHUNK])
                    total = edge if total is None else total + edge
                gathered[part, at] = total.astype(bf16)
            return carry

        lax.fori_loop(0, blocks, edges, 0)
        update = silu_of_half(own[part] + 0.5 * dot(gathered[part], w_gathered[layer]))
        projected = dot(update.astype(bf16), w_out[layer])
        center = jnp.mean(projected, axis=-1, keepdims=True)
        away = projected - center
        spread = jnp.mean(away * away, axis=-1, keepdims=True)
        normed = away * lax.rsqrt(spread + 1e-05) * norm_gain[layer : layer + 1]
        before = state[layer, part].reshape(rows, width).astype(f32)
        state[layer + 1, part] = (before + normed).astype(bf16).reshape(blocks, nodes, width)

    writes = []

    def decode(part):
        last = state[LAYERS, part].reshape(rows, width)
        table[part, :blocks] = (0.5 * dot(last, w_decode[...])).reshape(blocks, nodes, width)
        for g in range(grid_blocks):
            h = table[part, grid_links[g]] + 0.5 * encoded[part, g].astype(f32)
            encoded[part, g] = silu_of_half(h).astype(bf16)
        found = dot(encoded[part].reshape(grid_rows, width), w_final[...])
        out[part] = found.reshape(grid_blocks, nodes, -1)
        write = pltpu.make_async_copy(
            out.at[part], out_hbm.at[:, pl.ds(part * nodes, nodes)], out_sem.at[part]
        )
        write.start()
        writes.append(write)

    copies[0].wait()
    for part in range(PARTS):
        encode(part)
        if part == 0:
            pl.semaphore_wait(barrier, len(sides))
        ship(0, part)
    for number in (3, 6, 8):
        copies[number].wait()
    for layer in range(LAYERS):
        for number in (1, 2, 4):
            copies[layer, number].wait()
        for part in range(PARTS):
            project(layer, part)
        for number in (5, 7):
            copies[layer, number].wait()
        if layer == LAYERS - 1:
            copies[9].wait()
            copies[10].wait()
        for part in range(PARTS):
            process(layer, part)
            if layer + 1 < LAYERS:
                ship(layer + 1, part)
            else:
                decode(part)
    for write in writes:
        write.wait()
    for copy in sends.values():
        copy.wait_send()


def local(grid_in, mesh_static, block_links, grid_links, *weights):
    bf16, f32 = jnp.bfloat16, jnp.float32
    n = lax.axis_size("dom")
    rows, width = mesh_static.shape
    blocks = rows // BLOCK
    grid_rows, fields = grid_in.shape
    grid_blocks = grid_rows // BLOCK
    nodes = BLOCK // PARTS
    outputs = weights[-1].shape[1]
    scratch = [pltpu.VMEM(w.shape, w.dtype) for w in weights]
    scratch += [
        pltpu.VMEM((PARTS, grid_blocks, nodes, fields), bf16),
        pltpu.VMEM((PARTS, blocks, nodes, width), bf16),
        pltpu.VMEM((PARTS, grid_blocks, nodes, width), bf16),
        pltpu.VMEM((LAYERS + 1, PARTS, blocks, nodes, width), bf16),
        pltpu.VMEM((PARTS, blocks * nodes, width), f32),
        pltpu.VMEM((PARTS, blocks * nodes, width), f32),
        pltpu.VMEM((PARTS, blocks + REMOTE, nodes, width), f32),
        pltpu.VMEM((PARTS, blocks * nodes, width), bf16),
        pltpu.VMEM((LAYERS, PARTS, 2, CAP, nodes, width), bf16),
        pltpu.VMEM((LAYERS, PARTS, REMOTE, nodes, width), bf16),
        pltpu.VMEM((PARTS, grid_blocks, nodes, outputs), f32),
        pltpu.SMEM((blocks * K,), jnp.int32),
        pltpu.SemaphoreType.DMA((len(weights),)),
        pltpu.SemaphoreType.DMA((LAYERS, len(weights))),
        pltpu.SemaphoreType.DMA((PARTS,)),
        pltpu.SemaphoreType.DMA((PARTS,)),
        pltpu.SemaphoreType.DMA((PARTS,)),
        pltpu.SemaphoreType.DMA((LAYERS, PARTS, 4)),
        pltpu.SemaphoreType.DMA((LAYERS, PARTS, 4)),
    ]
    anywhere = pl.BlockSpec(memory_space=pl.ANY)
    in_hbm = pl.BlockSpec(memory_space=pltpu.HBM)
    found = pl.pallas_call(
        functools.partial(kernel, n, blocks, grid_blocks),
        out_shape=jax.ShapeDtypeStruct((grid_blocks, BLOCK, outputs), f32),
        in_specs=[pl.BlockSpec(memory_space=pltpu.SMEM)] * 2 + [in_hbm] * (2 + len(weights)),
        out_specs=anywhere,
        scratch_shapes=scratch,
        compiler_params=pltpu.CompilerParams(
            collective_id=0, has_side_effects=True, vmem_limit_bytes=24 * 1024 * 1024
        ),
    )(
        grid_links,
        block_links.T,
        grid_in.reshape(grid_blocks, BLOCK, fields),
        mesh_static.reshape(blocks, BLOCK, width),
        *weights,
    )
    return found.reshape(grid_rows, outputs)


def solution(mesh):
    whole = P()
    split = P(("groups", "dom"), None)
    in_specs = (split, P("dom", None), whole, P("dom")) + (whole,) * 11
    return jax.shard_map(
        local, mesh=mesh, in_specs=in_specs, out_specs=split, check_vma=False
    )
```
